32 devices in a mesh: row: 2 (over core), nbr: 4 (over y, x), feat: 4 (over z).
Axes of the slice: x: 2, y: 2, z: 4, core: 2. Of those that a mesh axis runs over, the one named last changes fastest.
Arguments:
- features: float32 [1024, 8192], P('feat', 'nbr'), may hold values from -6 to 6
- tile_list: int32 [2, 4, 2, 256], P('row', 'nbr'), may hold values from 0 to 15, as said below
- tile_count: int32 [2, 4], P('row', 'nbr'), may hold values from 96 to 256
- weight: float32 [1024, 1024], P(('row', 'nbr'), 'feat'), may hold values from -0.1875 to 0.1875
- cotangent: float32 [4096, 1024], P(('row', 'nbr'), 'feat'), may hold values from -6 to 6
Outputs:
- activations: float32 [4096, 1024], P(('row', 'nbr'), 'feat')
- feature_grad: float32 [1024, 8192], P('feat', 'nbr')
- weight_grad: float32 [1024, 1024], P(('row', 'nbr'), 'feat')
The draws below stay inside these ranges and needn't reach their ends.
Inputs may be any that keep to these rules, and one draw needn't show every extreme that they name: `tile_list`: each device's list names every (row block, column block) pair of its block exactly once; only the first tile_count entries are used.
All inputs are finite; a program needn't handle non-finite values.
Results may differ from the reference program's by a relative error of at most 0.0003.
Values sent between devices are 32-bit elements; how exact they have to be, the bound alone decides.
A program may use at most 64 MiB of HBM per device.

```python
import jax
import jax.numpy as jnp
from jax import lax

F = 1024
TILE = 128
R_DEV = 2048
C_DEV = 2048
TILE_MAX = 256
TILE_MIN = 96
ROWS = 4096
COLS = 8192
N_ROW = 2
N_NBR = 4


def draw_tile_count(key, part):
    key = jax.random.fold_in(key, 1)
    spread = max(TILE_MAX - TILE_MIN, 1)
    uniform_pick = jax.random.randint(key, (N_ROW, N_NBR), 0, TILE_MAX - TILE_MIN + 1)
    skewed = uniform_pick * uniform_pick // spread * uniform_pick // spread
    counts = TILE_MIN + skewed
    counts = counts.at[0, 0].set(TILE_MAX).at[1, 0].set(TILE_MIN)
    return counts.astype(jnp.int32)


def draw_tile_list(key, part):
    key = jax.random.fold_in(key, 2)
    device_keys = jax.random.split(key, N_ROW * N_NBR)

    def shuffled(single_key):
        return jax.random.permutation(single_key, TILE_MAX)
    orders = jax.vmap(shuffled)(device_keys).astype(jnp.int32)
    col_blocks = C_DEV // TILE
    stacked = jnp.stack([orders // col_blocks, orders % col_blocks], axis=1)
    return stacked.reshape(N_ROW, N_NBR, 2, TILE_MAX).astype(jnp.int32)


def shard_levels(key, shape, cuts, least, largest):
    factor_of, own = 1.0, jax.random.fold_in(key, 6)
    for dim, shards_of in cuts:
        steps = jnp.exp(jax.random.uniform(jax.random.fold_in(own, dim), (shards_of,), jnp.float32, least / len(cuts), largest / len(cuts)))
        factor_of = factor_of * jnp.repeat(steps, shape[dim] // shards_of).reshape([-1 if axis == dim else 1 for axis in range(len(shape))])
    return factor_of


def scatter_about(stream_key, extent, width, reach, pieces=(), held_as=jnp.bfloat16):
    factor_of = shard_levels(stream_key, extent, pieces, -0.22, 0.18) if pieces else 1.0
    values = jax.random.normal(stream_key, extent, jnp.float32) * width * factor_of
    return jnp.minimum(jnp.maximum(values, -reach), reach).astype(held_as)


def setup_inputs(seed: int = 0) -> dict:
    key_of = jax.random.split(jax.random.key(seed), 6)
    return {
        "features": scatter_about(key_of[0], (F, COLS), 1.0, 6.0, ((0, 4), (1, 4)), jnp.float32),
        "tile_list": draw_tile_list(jax.random.fold_in(key_of[5], 71), 0),
        "tile_count": draw_tile_count(jax.random.fold_in(key_of[5], 71), 0),
        "weight": scatter_about(key_of[3], (F, F), F ** -0.5, 0.1875, ((0, 8), (1, 4)), jnp.float32),
        "cotangent": scatter_about(key_of[4], (ROWS, F), 1.0, 6.0, ((0, 8), (1, 4)), jnp.float32),
    }


modulus = 32749
highest = lax.Precision.HIGHEST


def edge_value(row_index, col_index):
    hashed = ((row_index * row_index) % modulus * 3 + (col_index * col_index) % modulus * 5
              + (row_index * col_index) % modulus * 7 + row_index * 11 + col_index * 13) % modulus
    return hashed.astype(jnp.float32) / modulus - 0.5


def dense_block(tile_pairs, tile_total, row_id, nbr_id, edge_scale):
    slots = jnp.arange(TILE_MAX, dtype=jnp.int32)
    in_range = (slots < tile_total).astype(jnp.float32)
    row_onehot = (tile_pairs[0][:, None] == jnp.arange(R_DEV // TILE, dtype=jnp.int32)[None, :]).astype(jnp.float32) * in_range[:, None]
    col_onehot = (tile_pairs[1][:, None] == jnp.arange(C_DEV // TILE, dtype=jnp.int32)[None, :]).astype(jnp.float32)
    occupied = jnp.dot(row_onehot.T, col_onehot)
    occupied = jnp.repeat(jnp.repeat(occupied, TILE, axis=0), TILE, axis=1)
    rows_global = row_id * R_DEV + jnp.arange(R_DEV, dtype=jnp.int32)[:, None]
    cols_global = nbr_id * C_DEV + jnp.arange(C_DEV, dtype=jnp.int32)[None, :]
    return edge_value(rows_global, cols_global) * edge_scale * occupied


def reference(features, tile_list, tile_count, weight, cotangent):
    edge_scale = (12.0 / (C_DEV * N_NBR / 2)) ** 0.5
    blocks = features.T.reshape(N_NBR, C_DEV, F)
    nbr_ids = jnp.arange(N_NBR, dtype=jnp.int32)
    hidden_parts = []
    for row_id in range(N_ROW):
        def accumulate(running, items):
            nbr_id, block_x, pairs, totals = items
            adjacency = dense_block(pairs, totals, row_id, nbr_id, edge_scale)
            return running + jnp.dot(adjacency, block_x, precision=highest), None
        hidden_row, unused = lax.scan(accumulate, jnp.zeros((R_DEV, F), jnp.float32),
                                      (nbr_ids, blocks, tile_list[row_id], tile_count[row_id]))
        hidden_parts.append(hidden_row)
    hidden = jnp.concatenate(hidden_parts, axis=0)
    pre_act = jnp.dot(hidden, weight, precision=highest)
    squash = jax.nn.sigmoid(pre_act)
    activations = pre_act * squash
    grad_pre = cotangent * squash * (1.0 + pre_act * (1.0 - squash))
    grad_hidden = jnp.dot(grad_pre, weight.T, precision=highest)
    weight_grad = jnp.dot(hidden.T, grad_pre, precision=highest)
    grad_rows = grad_hidden.reshape(N_ROW, R_DEV, F)

    def column_block(carried, items):
        nbr_id, pairs, totals = items
        running = jnp.zeros((C_DEV, F), jnp.float32)
        for row_id in range(N_ROW):
            adjacency = dense_block(pairs[row_id], totals[row_id], row_id, nbr_id, edge_scale)
            running = running + jnp.dot(adjacency.T, grad_rows[row_id], precision=highest)
        return carried, running

    carried, stacked = lax.scan(column_block, jnp.zeros((), jnp.float32),
                                (nbr_ids, jnp.moveaxis(tile_list, 1, 0), tile_count.T))
    feature_grad = stacked.reshape(N_NBR * C_DEV, F).T
    return (activations, feature_grad, weight_grad)
```

```python
import functools

import jax
import jax.numpy as jnp
from jax import lax
from jax.experimental import pallas as pl
from jax.experimental.pallas import tpu as pltpu
from jax.sharding import PartitionSpec as P

TILE = 128
modulus = 32749
high = lax.Precision.HIGH
BF16, F32, I32 = jnp.bfloat16, jnp.float32, jnp.int32
VMEM_BYTES = 56 * 1024 * 1024


def mod_p(value):
    quotient = (value.astype(F32) * (1.0 / modulus)).astype(I32)
    rest = value - quotient * modulus
    rest = jnp.where(rest < 0, rest + modulus, rest)
    return jnp.where(rest >= modulus, rest - modulus, rest)


def halves(value):
    upper = value.astype(BF16)
    return upper, (value - upper.astype(F32)).astype(BF16)


def dot(a, b):
    return jnp.dot(a, b, preferred_element_type=F32)


def dot3(a_hi, a_lo, b_hi, b_lo):
    return dot(a_hi, b_hi) + (dot(a_hi, b_lo) + dot(a_lo, b_hi))


def edge_setup(row_id, nbr_id, pairs, total, row_part, col_part, inner, occupied):
    r_dev, c_dev = row_part.shape[0], inner.shape[1]
    row_blocks = r_dev // TILE
    slots = pairs.shape[1]
    r = row_id * r_dev + lax.broadcasted_iota(I32, (r_dev, TILE), 0)
    row_part[...] = mod_p(3 * r * r + 11 * r).astype(F32) - 1.5 * modulus
    c = nbr_id * c_dev + lax.broadcasted_iota(I32, (row_blocks, c_dev), 1)
    first = row_id * r_dev + TILE * lax.broadcasted_iota(I32, (row_blocks, c_dev), 0)
    columns = mod_p(5 * mod_p(c * c) + 13 * c + 7 * mod_p(first * c)).astype(F32)
    c = nbr_id * c_dev + lax.broadcasted_iota(I32, (TILE, c_dev), 1)
    i = lax.broadcasted_iota(I32, (TILE, c_dev), 0)
    inner[...] = mod_p(7 * i * c).astype(F32)
    listed = lax.broadcasted_iota(I32, (row_blocks, slots), 1) < total
    named = lax.broadcasted_iota(I32, (row_blocks, slots), 0) == pairs[0:1, :]
    row_hot = jnp.where(named & listed, 1.0, 0.0).astype(BF16)
    blocks = lax.broadcasted_iota(I32, (c_dev, slots), 0) // TILE
    col_hot = jnp.where(blocks == pairs[1:2, :], 1.0, 0.0).astype(BF16)
    tiles = lax.dot_general(
        row_hot, col_hot, (((1,), (1,)), ((), ())), preferred_element_type=F32
    )
    for block in range(row_blocks):
        col_part[block] = columns[block : block + 1, :]
        occupied[block] = tiles[block : block + 1, :]


def edge_rows(block, col, tables):
    row_part, col_part, inner, occupied = tables
    rows = pl.ds(pl.multiple_of(block * TILE, TILE), TILE)
    cols = pl.ds(col * TILE, TILE)
    total = row_part[rows, :] + (inner[:, cols] + col_part[block, :, cols])
    shift = jnp.where(
        total >= 0.5 * modulus, -1.0 * modulus, jnp.where(total < -0.5 * modulus, 1.0 * modulus, 0.0)
    )
    return halves((total + shift) * occupied[block, :, cols])


def fill(slot_hi, slot_lo, block, offset, tables):
    for col in range(slot_hi.shape[1] // TILE):
        upper, lower = edge_rows(block, col, tables)
        slot_hi[offset : offset + TILE, col * TILE : (col + 1) * TILE] = upper
        slot_lo[offset : offset + TILE, col * TILE : (col + 1) * TILE] = lower


def table_shapes(r_dev, c_dev):
    blocks = r_dev // TILE
    return [
        pltpu.VMEM((r_dev, TILE), F32),
        pltpu.VMEM((blocks, 1, c_dev), F32),
        pltpu.VMEM((TILE, c_dev), F32),
        pltpu.VMEM((blocks, 1, c_dev), F32),
    ]


def forward_kernel(scale, ids, total, pairs, x, out, x_hi, x_lo, a_hi, a_lo, *tables):
    edge_setup(ids[0], ids[1], pairs, total[0], *tables)
    upper, lower = halves(x[...].T)
    x_hi[...] = upper
    x_lo[...] = lower
    step = a_hi.shape[0]

    def advance(chunk, carry):
        for part in range(step // TILE):
            fill(a_hi, a_lo, chunk * (step // TILE) + part, part * TILE, tables)
        rows = pl.ds(pl.multiple_of(chunk * step, step), step)
        out[rows, :] = scale * dot3(a_hi[...], a_lo[...], x_hi[...], x_lo[...])
        return carry

    lax.fori_loop(0, out.shape[0] // step, advance, 0)


def backward_kernel(scale, ids, total, pairs, grad, out, a_hi, a_lo, *tables):
    edge_setup(ids[0], ids[1], pairs, total[0], *tables)
    step = a_hi.shape[0]
    out[...] = jnp.zeros_like(out)

    def advance(chunk, carry):
        for part in range(step // TILE):
            fill(a_hi, a_lo, chunk * (step // TILE) + part, part * TILE, tables)
        rows = pl.ds(pl.multiple_of(chunk * step, step), step)
        g_hi, g_lo = halves(grad[rows, :].T * scale)
        out[...] += dot3(g_hi, g_lo, a_hi[...], a_lo[...])
        return carry

    lax.fori_loop(0, grad.shape[0] // step, advance, 0)


def local_call(kernel, out_shape, scratch, args, flops):
    smem = pl.BlockSpec(memory_space=pltpu.SMEM)
    vmem = pl.BlockSpec(memory_space=pltpu.VMEM)
    return pl.pallas_call(
        kernel,
        out_shape=jax.ShapeDtypeStruct(out_shape, F32),
        in_specs=[smem, smem, vmem, vmem],
        out_specs=vmem,
        scratch_shapes=scratch,
        compiler_params=pltpu.CompilerParams(vmem_limit_bytes=VMEM_BYTES),
        cost_estimate=pl.CostEstimate(flops=flops, bytes_accessed=4 << 20, transcendentals=0),
    )(*args)


def per_device(features, tile_list, tile_count, weight, cotangent):
    pairs = tile_list[0, 0]
    n_nbr = lax.axis_size("nbr")
    width, c_dev = features.shape
    r_dev = cotangent.shape[0] * n_nbr
    scale = (12.0 / (c_dev * n_nbr / 2)) ** 0.5 / modulus
    ids = jnp.stack([lax.axis_index("row"), lax.axis_index("nbr")]).astype(I32)
    total = tile_count[0]
    tables = table_shapes(r_dev, c_dev)
    flops = 6 * r_dev * c_dev * width
    adjacency = [pltpu.VMEM((256, c_dev), BF16)] * 2
    partial_value = local_call(
        functools.partial(forward_kernel, scale),
        (r_dev, width),
        [pltpu.VMEM((c_dev, width), BF16)] * 2 + adjacency + tables,
        (ids, total, pairs, features),
        flops,
    )
    hidden = lax.psum_scatter(partial_value, "nbr", scatter_dimension=0, tiled=True)
    weight_cols = lax.all_gather(weight, ("row", "nbr"), axis=0, tiled=True)
    hidden_all = lax.all_gather(hidden, "feat", axis=1, tiled=True)
    pre_act = jnp.dot(hidden_all, weight_cols, precision=high)
    squash = jax.nn.sigmoid(pre_act)
    activations = pre_act * squash
    grad_pre = cotangent * squash * (1.0 + pre_act * (1.0 - squash))
    grad_hidden = lax.psum_scatter(
        jnp.dot(grad_pre, weight_cols.T, precision=high), "feat", scatter_dimension=1, tiled=True
    )
    weight_terms = jnp.dot(hidden_all.T, grad_pre, precision=high)
    weight_grad = lax.psum_scatter(weight_terms, ("row", "nbr"), scatter_dimension=0, tiled=True)
    grad_block = lax.all_gather(grad_hidden, "nbr", axis=0, tiled=True)
    column_part = local_call(
        functools.partial(backward_kernel, scale),
        (width, c_dev),
        adjacency + tables,
        (ids, total, pairs, grad_block),
        flops,
    )
    feature_grad = lax.psum(column_part, "row")
    return (activations, feature_grad, weight_grad)


def solution(mesh):
    in_specs = (
        P("feat", "nbr"),
        P("row", "nbr", None, None),
        P("row", "nbr"),
        P(("row", "nbr"), "feat"),
        P(("row", "nbr"), "feat"),
    )
    out_specs = (P(("row", "nbr"), "feat"), P("feat", "nbr"), P(("row", "nbr"), "feat"))
    return jax.shard_map(
        per_device, mesh=mesh, in_specs=in_specs, out_specs=out_specs, check_vma=False
    )
```

```python
import functools

import jax
import jax.numpy as jnp
from jax import lax
from jax.experimental import pallas as pl
from jax.experimental.pallas import tpu as pltpu
from jax.sharding import PartitionSpec as P

TILE = 128
modulus = 32749
high = lax.Precision.HIGH
BF16, F32, I32 = jnp.bfloat16, jnp.float32, jnp.int32
VMEM_BYTES = 56 * 1024 * 1024


def mod_p(value):
    quotient = (value.astype(F32) * (1.0 / modulus)).astype(I32)
    rest = value - quotient * modulus
    rest = jnp.where(rest < 0, rest + modulus, rest)
    return jnp.where(rest >= modulus, rest - modulus, rest)


def halves(value):
    upper = value.astype(BF16)
    return upper, (value - upper.astype(F32)).astype(BF16)


def dot(a, b):
    return jnp.dot(a, b, preferred_element_type=F32)


def dot3(a_hi, a_lo, b_hi, b_lo):
    return dot(a_hi, b_hi) + (dot(a_hi, b_lo) + dot(a_lo, b_hi))


def edge_setup(row_id, nbr_id, pairs, total, row_part, col_part, inner, occupied):
    r_dev, c_dev = row_part.shape[0], inner.shape[1]
    row_blocks = r_dev // TILE
    slots = pairs.shape[1]
    r = row_id * r_dev + lax.broadcasted_iota(I32, (r_dev, TILE), 0)
    row_part[...] = mod_p(3 * r * r + 11 * r).astype(F32) - 1.5 * modulus
    c = nbr_id * c_dev + lax.broadcasted_iota(I32, (row_blocks, c_dev), 1)
    first = row_id * r_dev + TILE * lax.broadcasted_iota(I32, (row_blocks, c_dev), 0)
    columns = mod_p(5 * mod_p(c * c) + 13 * c + 7 * mod_p(first * c)).astype(F32)
    c = nbr_id * c_dev + lax.broadcasted_iota(I32, (TILE, c_dev), 1)
    i = lax.broadcasted_iota(I32, (TILE, c_dev), 0)
    inner[...] = mod_p(7 * i * c).astype(F32)
    listed = lax.broadcasted_iota(I32, (row_blocks, slots), 1) < total
    named = lax.broadcasted_iota(I32, (row_blocks, slots), 0) == pairs[0:1, :]
    row_hot = jnp.where(named & listed, 1.0, 0.0).astype(BF16)
    blocks = lax.broadcasted_iota(I32, (c_dev, slots), 0) // TILE
    col_hot = jnp.where(blocks == pairs[1:2, :], 1.0, 0.0).astype(BF16)
    tiles = lax.dot_general(
        row_hot, col_hot, (((1,), (1,)), ((), ())), preferred_element_type=F32
    )
    for block in range(row_blocks):
        col_part[block] = columns[block : block + 1, :]
        occupied[block] = tiles[block : block + 1, :]


def edge_rows(block, col, tables):
    row_part, col_part, inner, occupied = tables
    rows = pl.ds(pl.multiple_of(block * TILE, TILE), TILE)
    cols = pl.ds(col * TILE, TILE)
    total = row_part[rows, :] + (inner[:, cols] + col_part[block, :, cols])
    shift = jnp.where(
        total >= 0.5 * modulus, -1.0 * modulus, jnp.where(total < -0.5 * modulus, 1.0 * modulus, 0.0)
    )
    return halves((total + shift) * occupied[block, :, cols])


def fill(slot_hi, slot_lo, block, offset, tables):
    for col in range(slot_hi.shape[1] // TILE):
        upper, lower = edge_rows(block, col, tables)
        slot_hi[offset : offset + TILE, col * TILE : (col + 1) * TILE] = upper
        slot_lo[offset : offset + TILE, col * TILE : (col + 1) * TILE] = lower


def table_shapes(r_dev, c_dev):
    blocks = r_dev // TILE
    return [
        pltpu.VMEM((r_dev, TILE), F32),
        pltpu.VMEM((blocks, 1, c_dev), F32),
        pltpu.VMEM((TILE, c_dev), F32),
        pltpu.VMEM((blocks, 1, c_dev), F32),
    ]


def forward_kernel(scale, ids, total, pairs, x, out, x_hi, x_lo, a_hi, a_lo, *tables):
    edge_setup(ids[0], ids[1], pairs, total[0], *tables)
    upper, lower = halves(x[...].T)
    x_hi[...] = upper
    x_lo[...] = lower
    step = a_hi.shape[0]

    def advance(chunk, carry):
        for part in range(step // TILE):
            fill(a_hi, a_lo, chunk * (step // TILE) + part, part * TILE, tables)
        rows = pl.ds(pl.multiple_of(chunk * step, step), step)
        out[rows, :] = scale * dot3(a_hi[...], a_lo[...], x_hi[...], x_lo[...])
        return carry

    lax.fori_loop(0, out.shape[0] // step, advance, 0)


def backward_kernel(scale, ids, total, pairs, grad, out, a_hi, a_lo, *tables):
    edge_setup(ids[0], ids[1], pairs, total[0], *tables)
    step = a_hi.shape[0]
    out[...] = jnp.zeros_like(out)

    def advance(chunk, carry):
        for part in range(step // TILE):
            fill(a_hi, a_lo, chunk * (step // TILE) + part, part * TILE, tables)
        rows = pl.ds(pl.multiple_of(chunk * step, step), step)
        g_hi, g_lo = halves(grad[rows, :].T * scale)
        out[...] += dot3(g_hi, g_lo, a_hi[...], a_lo[...])
        return carry

    lax.fori_loop(0, grad.shape[0] // step, advance, 0)


def local_call(kernel, out_shape, scratch, args, flops):
    smem = pl.BlockSpec(memory_space=pltpu.SMEM)
    vmem = pl.BlockSpec(memory_space=pltpu.VMEM)
    return pl.pallas_call(
        kernel,
        out_shape=jax.ShapeDtypeStruct(out_shape, F32),
        in_specs=[smem, smem, vmem, vmem],
        out_specs=vmem,
        scratch_shapes=scratch,
        compiler_params=pltpu.CompilerParams(vmem_limit_bytes=VMEM_BYTES),
        cost_estimate=pl.CostEstimate(flops=flops, bytes_accessed=4 << 20, transcendentals=0),
    )(*args)


MESH = pl.DeviceIdType.MESH
CHUNKS = 4


def fused_kernel(
    scale, total, pairs, x, w, cot,
    act, own_out, other_out, wg_out,
    x_hi, x_lo, a_hi, a_lo, part, dx, dy, rx, ry, h, h_hi, h_lo, gp, rl, rr, ga,
    wall, w_hi, w_lo, wt_hi, wt_lo, wterm, wpeer, wsum, wrecv,
    d_s, d_r, p_s, p_r, ag_s, ag_r, rs_s, rs_r, t_s, t_r,
    w_s, w_r, wp_s, wp_r, wg_s, wg_r, out_s, out_r, *tables,
):
    row, n, z = lax.axis_index("row"), lax.axis_index("nbr"), lax.axis_index("feat")
    col, line = lax.rem(n, 2), n // 2
    nx, ny, nd = line * 2 + (1 - col), (1 - line) * 2 + col, 3 - n
    peer = 1 - row
    right, left = jnp.minimum(z + 1, 3), jnp.maximum(z - 1, 0)
    half = TILE // 2
    owners = (nd, nx, ny, n)

    def send(src, dst, s_sem, r_sem, **to):
        return pltpu.make_async_remote_copy(
            src_ref=src, dst_ref=dst, send_sem=s_sem, recv_sem=r_sem,
            device_id=to, device_id_type=MESH,
        )

    def copy_diag(k, way):
        rows = pl.ds(way * half, half)
        return send(part.at[k, 0, rows], (dx, dy)[way].at[k], d_s.at[k, way], d_r.at[k, way],
                    nbr=(nx, ny)[way])

    def copy_part(k, way):
        return send(part.at[k, 1 + way], (rx, ry)[way].at[k], p_s.at[k, way], p_r.at[k, way],
                    nbr=(nx, ny)[way])

    def copy_hidden(k, block, step, way):
        return send(h.at[k, block], h.at[k, block], ag_s.at[k, way * 3 + step], ag_r.at[k, block],
                    feat=(right, left)[way])

    def copy_sum(k, block, step, way):
        buffer = (rl, rr)[way]
        return send(buffer.at[k, block], buffer.at[k, block], rs_s.at[k, way * 3 + step],
                    rs_r.at[k, way * 4 + block], feat=(right, left)[way])

    def copy_grad(k, way):
        return send(ga.at[k, 3], ga.at[k, 1 + way], t_s.at[k, way], t_r.at[k, way], nbr=(nx, ny)[way])

    def copy_on(k, way):
        rows = pl.ds(way * half, half)
        return send(ga.at[k, 1 + way, rows], ga.at[k, 0, rows], t_s.at[k, 2 + way], t_r.at[k, 2 + way],
                    nbr=(ny, nx)[way])

    def copy_weight(j, source):
        return send(w, wall.at[row * 4 + source], w_s.at[j], w_r.at[source], nbr=owners[j])

    def copy_weight_peer(m, side):
        return send(wall.at[side * 4 + m], wall.at[side * 4 + m], wp_s.at[m], wp_r.at[m], row=peer)

    def copy_terms():
        return send(wterm.at[pl.ds(peer * 4, 4)], wpeer, wg_s.at[3], wg_r.at[4], row=peer)

    def copy_wsum(j, source):
        return send(wsum.at[owners[j]], wrecv.at[source], wg_s.at[j], wg_r.at[source], nbr=owners[j])

    piece = own_out.shape[1] // 4

    def copy_out(j):
        cols = pl.ds(j * piece, piece)
        return send(own_out.at[:, cols], other_out.at[:, cols], out_s.at[j], out_r.at[j], row=peer)

    barrier = pltpu.get_barrier_semaphore()
    for target in (nx, ny, nd):
        pl.semaphore_signal(barrier, inc=1, device_id={"nbr": target}, device_id_type=MESH)
    pl.semaphore_signal(barrier, inc=1, device_id={"row": peer}, device_id_type=MESH)

    @pl.when(z > 0)
    def _():
        pl.semaphore_signal(barrier, inc=1, device_id={"feat": left}, device_id_type=MESH)

    @pl.when(z < 3)
    def _():
        pl.semaphore_signal(barrier, inc=1, device_id={"feat": right}, device_id_type=MESH)

    edge_setup(row, n, pairs, total[0], *tables)
    upper, lower = halves(x[...].T)
    x_hi[...] = upper
    x_lo[...] = lower
    wall[row * 4 + n] = w[...]
    wterm[...] = jnp.zeros_like(wterm)
    own_out[...] = jnp.zeros_like(own_out)
    pl.semaphore_wait(barrier, 4 + jnp.where(z > 0, 1, 0) + jnp.where(z < 3, 1, 0))
    for j in range(3):
        copy_weight(j, n).start()

    def product(k, side):
        for slot in (2 * side, 2 * side + 1):
            fill(a_hi.at[k], a_lo.at[k], owners[slot] * CHUNKS + k, slot * TILE, tables)
        rows = pl.ds(2 * side * TILE, 2 * TILE)
        value = dot3(a_hi[k, rows, :], a_lo[k, rows, :], x_hi[...], x_lo[...])
        part[k, 2 * side] = value[:TILE]
        part[k, 2 * side + 1] = value[TILE:]

    def gather_step(k, step):
        @pl.when(z >= step)
        def _():
            copy_hidden(k, z - step, 0, 0).wait_recv()
            if step < 3:
                @pl.when(z < 3)
                def _():
                    copy_hidden(k, z - step, step, 0).start()

        @pl.when(z <= 3 - step)
        def _():
            copy_hidden(k, z + step, 0, 1).wait_recv()
            if step < 3:
                @pl.when(z > 0)
                def _():
                    copy_hidden(k, z + step, step, 1).start()

    def sum_step(k, step):
        @pl.when((z >= 1) & (z <= 2) & (z <= step))
        def _():
            block = 3 - step + z
            copy_sum(k, block, 0, 0).wait_recv()
            rl[k, block] += gp[block]
            copy_sum(k, block, step - z, 0).start()

        @pl.when((z >= 1) & (z <= 2) & (3 - z <= step))
        def _():
            block = step + z - 3
            copy_sum(k, block, 0, 1).wait_recv()
            rr[k, block] += gp[block]
            copy_sum(k, block, step - 3 + z, 1).start()

    def dense(k):
        rows = pl.ds(pl.multiple_of(k * TILE, TILE), TILE)
        wide = h_hi.shape[1] // 4
        for block in range(4):
            cols = slice(block * wide, (block + 1) * wide)
            h_hi[:, cols], h_lo[:, cols] = halves(h[k, block])
        pre = dot3(h_hi[...], h_lo[...], w_hi[...], w_lo[...])
        squash = jax.nn.sigmoid(pre)
        act[rows, :] = pre * squash
        grad_pre = cot[rows, :] * squash * (1.0 + pre * (1.0 - squash))
        g_hi, g_lo = halves(grad_pre)
        terms = dot3(g_hi, g_lo, wt_hi[...], wt_lo[...])
        for block in range(4):
            gp[block] = terms[:, block * wide : (block + 1) * wide]

        @pl.when(z == 0)
        def _():
            for step in range(3):
                rl[k, 3 - step] = gp[3 - step]
                copy_sum(k, 3 - step, step, 0).start()

        @pl.when(z == 3)
        def _():
            for step in range(3):
                rr[k, step] = gp[step]
                copy_sum(k, step, step, 1).start()

        g_hi, g_lo = halves(grad_pre.T)
        terms = dot3(g_hi, g_lo, h_hi[...], h_lo[...])
        for block in range(8):
            wterm[block] += terms[:, block * TILE : (block + 1) * TILE]

    def advance(turn, carry):
        f, m, s, b = turn, turn - 1, turn - 2, turn - 3
        do_f, do_m = turn < 4, (turn >= 1) & (turn < 5)
        do_s, do_b = (turn >= 2) & (turn < 6), turn >= 3

        @pl.when(do_f)
        def _():
            product(f, 0)
            copy_diag(f, 0).start()
            copy_diag(f, 1).start()

        @pl.when(do_m)
        def _():
            gather_step(m, 1)

        @pl.when(do_s)
        def _():
            sum_step(s, 1)

        @pl.when(do_b)
        def _():
            for way in range(2):
                copy_grad(b, way).wait_recv()
                copy_on(b, way).start()

        @pl.when(do_f)
        def _():
            product(f, 1)
            for way in range(2):
                copy_diag(f, way).wait_recv()
            part[f, 1, half:, :] += dy[f]
            copy_part(f, 0).start()
            part[f, 2, :half, :] += dx[f]
            copy_part(f, 1).start()

        @pl.when(do_m)
        def _():
            gather_step(m, 2)

        @pl.when(do_s)
        def _():
            sum_step(s, 2)

        @pl.when(turn == 0)
        def _():
            copy_weight_peer(n, row).start()
            for j in range(3):
                copy_weight(j, owners[j]).wait_recv()
                copy_weight_peer(owners[j], row).start()

        @pl.when(do_f)
        def _():
            for way in range(2):
                copy_part(f, way).wait_recv()
            h[f, z] = (part[f, 3] + rx[f] + ry[f]) * scale

            @pl.when(z < 3)
            def _():
                copy_hidden(f, z, 0, 0).start()

            @pl.when(z > 0)
            def _():
                copy_hidden(f, z, 0, 1).start()

        @pl.when(turn == 0)
        def _():
            for m_ in range(4):
                copy_weight_peer(m_, peer).wait_recv()
            whole = wall[...].reshape(w_hi.shape)
            w_hi[...], w_lo[...] = halves(whole)
            wt_hi[...], wt_lo[...] = halves(whole.T)

        @pl.when(do_s)
        def _():
            ga[s, 3] = gp[z]

            @pl.when(z > 0)
            def _():
                copy_sum(s, z, 0, 0).wait_recv()
                ga[s, 3] += rl[s, z]

            @pl.when(z < 3)
            def _():
                copy_sum(s, z, 0, 1).wait_recv()
                ga[s, 3] += rr[s, z]

            for way in range(2):
                copy_grad(s, way).start()

        @pl.when(do_m)
        def _():
            gather_step(m, 3)
            dense(m)

        @pl.when(turn == 4)
        def _():
            copy_terms().start()

        @pl.when(turn == 5)
        def _():
            copy_terms().wait_recv()
            wsum[...] = wterm[pl.ds(row * 4, 4)] + wpeer[...]
            for j in range(3):
                copy_wsum(j, n).start()

        @pl.when(do_b)
        def _():
            for way in range(2):
                copy_on(b, way).wait_recv()
            grads = ga[b].reshape(CHUNKS * TILE, ga.shape[3])
            g_hi, g_lo = halves(grads.T * scale)
            for j in range(4):
                cols = slice(j * piece, (j + 1) * piece)
                own_out[:, cols] += dot3(g_hi, g_lo, a_hi[b, :, cols], a_lo[b, :, cols])

                @pl.when(turn == 6)
                def _():
                    copy_out(j).start()

        return carry

    lax.fori_loop(0, 7, advance, 0)

    for j in range(3):
        copy_wsum(j, owners[j]).wait_recv()
    wg_out[...] = (wsum[n] + wrecv[nx] + wrecv[ny] + wrecv[nd]).T
    for j in range(3):
        copy_weight(j, n).wait_send()
        copy_wsum(j, n).wait_send()
    copy_terms().wait_send()
    for m_ in range(4):
        copy_weight_peer(m_, row).wait_send()

    def settle(k, carry):
        for way in range(2):
            copy_diag(k, way).wait_send()
            copy_part(k, way).wait_send()
            copy_grad(k, way).wait_send()
            copy_on(k, way).wait_send()
        for step in range(3):
            @pl.when((z >= step) & (z < 3))
            def _():
                copy_hidden(k, z - step, step, 0).wait_send()

            @pl.when((z <= 3 - step) & (z > 0))
            def _():
                copy_hidden(k, z + step, step, 1).wait_send()

            @pl.when(step < 3 - z)
            def _():
                copy_sum(k, 3, step, 0).wait_send()

            @pl.when(step < z)
            def _():
                copy_sum(k, 0, step, 1).wait_send()
        return carry

    lax.fori_loop(0, CHUNKS, settle, 0)
    for j in range(4):
        copy_out(j).wait_send()
        copy_out(j).wait_recv()


def fused(features, pairs, total, weight, cotangent, scale):
    width, c_dev = features.shape
    full = 4 * width
    r_dev = cotangent.shape[0] * 4
    block = (CHUNKS, 4, TILE, width)
    smem = pl.BlockSpec(memory_space=pltpu.SMEM)
    vmem = pl.BlockSpec(memory_space=pltpu.VMEM)
    dma = pltpu.SemaphoreType.DMA
    scratch = [
        pltpu.VMEM((c_dev, width), BF16), pltpu.VMEM((c_dev, width), BF16),
        pltpu.VMEM((CHUNKS, 4 * TILE, c_dev), BF16), pltpu.VMEM((CHUNKS, 4 * TILE, c_dev), BF16),
        pltpu.VMEM(block, F32),
        pltpu.VMEM((CHUNKS, TILE // 2, width), F32), pltpu.VMEM((CHUNKS, TILE // 2, width), F32),
        pltpu.VMEM((CHUNKS, TILE, width), F32), pltpu.VMEM((CHUNKS, TILE, width), F32),
        pltpu.VMEM(block, F32),
        pltpu.VMEM((TILE, full), BF16), pltpu.VMEM((TILE, full), BF16),
        pltpu.VMEM(block[1:], F32),
        pltpu.VMEM(block, F32), pltpu.VMEM(block, F32), pltpu.VMEM(block, F32),
        pltpu.VMEM((8, full // 8, width), F32),
        pltpu.VMEM((full, width), BF16), pltpu.VMEM((full, width), BF16),
        pltpu.VMEM((width, full), BF16), pltpu.VMEM((width, full), BF16),
        pltpu.VMEM((8, width, full // 8), F32),
        pltpu.VMEM((4, width, full // 8), F32), pltpu.VMEM((4, width, full // 8), F32),
        pltpu.VMEM((4, width, full // 8), F32),
        dma((CHUNKS, 2)), dma((CHUNKS, 2)), dma((CHUNKS, 2)), dma((CHUNKS, 2)),
        dma((CHUNKS, 6)), dma((CHUNKS, 4)), dma((CHUNKS, 6)), dma((CHUNKS, 8)),
        dma((CHUNKS, 4)), dma((CHUNKS, 4)),
        dma((3,)), dma((4,)), dma((4,)), dma((4,)), dma((4,)), dma((5,)), dma((4,)), dma((4,)),
    ] + table_shapes(r_dev, c_dev)
    shape = lambda *dims: jax.ShapeDtypeStruct(dims, F32)
    act, own, other, wg = pl.pallas_call(
        functools.partial(fused_kernel, scale),
        out_shape=[shape(*cotangent.shape), shape(width, c_dev), shape(width, c_dev), shape(*weight.shape)],
        in_specs=[smem, vmem, vmem, vmem, vmem],
        out_specs=[vmem, vmem, pl.BlockSpec(memory_space=pl.ANY), vmem],
        scratch_shapes=scratch,
        compiler_params=pltpu.CompilerParams(
            collective_id=0, has_side_effects=True, vmem_limit_bytes=VMEM_BYTES
        ),
        cost_estimate=pl.CostEstimate(
            flops=12 * r_dev * c_dev * width, bytes_accessed=16 << 20, transcendentals=cotangent.size
        ),
    )(total, pairs, features, weight, cotangent)
    return act, own + other, wg


def per_device(features, tile_list, tile_count, weight, cotangent):
    pairs = tile_list[0, 0]
    n_nbr = lax.axis_size("nbr")
    width, c_dev = features.shape
    r_dev = cotangent.shape[0] * n_nbr
    scale = (12.0 / (c_dev * n_nbr / 2)) ** 0.5 / modulus
    ids = jnp.stack([lax.axis_index("row"), lax.axis_index("nbr")]).astype(I32)
    total = tile_count[0]
    sizes = (lax.axis_size("row"), n_nbr, lax.axis_size("feat"))
    if sizes == (2, 4, 4) and width % TILE == 0 and r_dev == 16 * TILE and weight.shape[0] == TILE:
        return fused(features, pairs, total, weight, cotangent, scale)
    tables = table_shapes(r_dev, c_dev)
    flops = 6 * r_dev * c_dev * width
    adjacency = [pltpu.VMEM((256, c_dev), BF16)] * 2
    partial_value = local_call(
        functools.partial(forward_kernel, scale),
        (r_dev, width),
        [pltpu.VMEM((c_dev, width), BF16)] * 2 + adjacency + tables,
        (ids, total, pairs, features),
        flops,
    )
    hidden = lax.psum_scatter(partial_value, "nbr", scatter_dimension=0, tiled=True)
    weight_cols = lax.all_gather(weight, ("row", "nbr"), axis=0, tiled=True)
    hidden_all = lax.all_gather(hidden, "feat", axis=1, tiled=True)
    pre_act = jnp.dot(hidden_all, weight_cols, precision=high)
    squash = jax.nn.sigmoid(pre_act)
    activations = pre_act * squash
    grad_pre = cotangent * squash * (1.0 + pre_act * (1.0 - squash))
    grad_hidden = lax.psum_scatter(
        jnp.dot(grad_pre, weight_cols.T, precision=high), "feat", scatter_dimension=1, tiled=True
    )
    weight_terms = jnp.dot(hidden_all.T, grad_pre, precision=high)
    weight_grad = lax.psum_scatter(weight_terms, ("row", "nbr"), scatter_dimension=0, tiled=True)
    grad_block = lax.all_gather(grad_hidden, "nbr", axis=0, tiled=True)
    column_part = local_call(
        functools.partial(backward_kernel, scale),
        (width, c_dev),
        adjacency + tables,
        (ids, total, pairs, grad_block),
        flops,
    )
    feature_grad = lax.psum(column_part, "row")
    return (activations, feature_grad, weight_grad)


def solution(mesh):
    in_specs = (
        P("feat", "nbr"),
        P("row", "nbr", None, None),
        P("row", "nbr"),
        P(("row", "nbr"), "feat"),
        P(("row", "nbr"), "feat"),
    )
    out_specs = (P(("row", "nbr"), "feat"), P("feat", "nbr"), P(("row", "nbr"), "feat"))
    return jax.shard_map(
        per_device, mesh=mesh, in_specs=in_specs, out_specs=out_specs, check_vma=False
    )
```

```python
import functools

import jax
import jax.numpy as jnp
from jax import lax
from jax.experimental import pallas as pl
from jax.experimental.pallas import tpu as pltpu
from jax.sharding import PartitionSpec as P

TILE = 128
modulus = 32749
high = lax.Precision.HIGH
BF16, F32, I32 = jnp.bfloat16, jnp.float32, jnp.int32
VMEM_BYTES = 56 * 1024 * 1024


def mod_p(value):
    quotient = (value.astype(F32) * (1.0 / modulus)).astype(I32)
    rest = value - quotient * modulus
    rest = jnp.where(rest < 0, rest + modulus, rest)
    return jnp.where(rest >= modulus, rest - modulus, rest)


def halves(value):
    upper = value.astype(BF16)
    return upper, (value - upper.astype(F32)).astype(BF16)


def dot(a, b):
    return jnp.dot(a, b, preferred_element_type=F32)


def dot3(a_hi, a_lo, b_hi, b_lo):
    return dot(a_hi, b_hi) + (dot(a_hi, b_lo) + dot(a_lo, b_hi))


def edge_setup(row_id, nbr_id, pairs, total, row_part, col_part, inner, occupied):
    r_dev, c_dev = row_part.shape[0], inner.shape[1]
    row_blocks = r_dev // TILE
    slots = pairs.shape[1]
    r = row_id * r_dev + lax.broadcasted_iota(I32, (r_dev, TILE), 0)
    row_part[...] = mod_p(3 * r * r + 11 * r).astype(F32) - 1.5 * modulus
    c = nbr_id * c_dev + lax.broadcasted_iota(I32, (row_blocks, c_dev), 1)
    first = row_id * r_dev + TILE * lax.broadcasted_iota(I32, (row_blocks, c_dev), 0)
    columns = mod_p(5 * mod_p(c * c) + 13 * c + 7 * mod_p(first * c)).astype(F32)
    c = nbr_id * c_dev + lax.broadcasted_iota(I32, (TILE, c_dev), 1)
    i = lax.broadcasted_iota(I32, (TILE, c_dev), 0)
    inner[...] = mod_p(7 * i * c).astype(F32)
    listed = lax.broadcasted_iota(I32, (row_blocks, slots), 1) < total
    named = lax.broadcasted_iota(I32, (row_blocks, slots), 0) == pairs[0:1, :]
    row_hot = jnp.where(named & listed, 1.0, 0.0).astype(BF16)
    blocks = lax.broadcasted_iota(I32, (c_dev, slots), 0) // TILE
    col_hot = jnp.where(blocks == pairs[1:2, :], 1.0, 0.0).astype(BF16)
    tiles = lax.dot_general(
        row_hot, col_hot, (((1,), (1,)), ((), ())), preferred_element_type=F32
    )
    for block in range(row_blocks):
        col_part[block] = columns[block : block + 1, :]
        occupied[block] = tiles[block : block + 1, :]


def edge_rows(block, col, tables):
    row_part, col_part, inner, occupied = tables
    rows = pl.ds(pl.multiple_of(block * TILE, TILE), TILE)
    cols = pl.ds(col * TILE, TILE)
    total = row_part[rows, :] + (inner[:, cols] + col_part[block, :, cols])
    shift = jnp.where(
        total >= 0.5 * modulus, -1.0 * modulus, jnp.where(total < -0.5 * modulus, 1.0 * modulus, 0.0)
    )
    return halves((total + shift) * occupied[block, :, cols])


def fill(slot_hi, slot_lo, block, offset, tables):
    for col in range(slot_hi.shape[1] // TILE):
        upper, lower = edge_rows(block, col, tables)
        slot_hi[offset : offset + TILE, col * TILE : (col + 1) * TILE] = upper
        slot_lo[offset : offset + TILE, col * TILE : (col + 1) * TILE] = lower


def table_shapes(r_dev, c_dev):
    blocks = r_dev // TILE
    return [
        pltpu.VMEM((r_dev, TILE), F32),
        pltpu.VMEM((blocks, 1, c_dev), F32),
        pltpu.VMEM((TILE, c_dev), F32),
        pltpu.VMEM((blocks, 1, c_dev), F32),
    ]


def forward_kernel(scale, ids, total, pairs, x, out, x_hi, x_lo, a_hi, a_lo, *tables):
    edge_setup(ids[0], ids[1], pairs, total[0], *tables)
    upper, lower = halves(x[...].T)
    x_hi[...] = upper
    x_lo[...] = lower
    step = a_hi.shape[0]

    def advance(chunk, carry):
        for part in range(step // TILE):
            fill(a_hi, a_lo, chunk * (step // TILE) + part, part * TILE, tables)
        rows = pl.ds(pl.multiple_of(chunk * step, step), step)
        out[rows, :] = scale * dot3(a_hi[...], a_lo[...], x_hi[...], x_lo[...])
        return carry

    lax.fori_loop(0, out.shape[0] // step, advance, 0)


def backward_kernel(scale, ids, total, pairs, grad, out, a_hi, a_lo, *tables):
    edge_setup(ids[0], ids[1], pairs, total[0], *tables)
    step = a_hi.shape[0]
    out[...] = jnp.zeros_like(out)

    def advance(chunk, carry):
        for part in range(step // TILE):
            fill(a_hi, a_lo, chunk * (step // TILE) + part, part * TILE, tables)
        rows = pl.ds(pl.multiple_of(chunk * step, step), step)
        g_hi, g_lo = halves(grad[rows, :].T * scale)
        out[...] += dot3(g_hi, g_lo, a_hi[...], a_lo[...])
        return carry

    lax.fori_loop(0, grad.shape[0] // step, advance, 0)


def local_call(kernel, out_shape, scratch, args, flops):
    smem = pl.BlockSpec(memory_space=pltpu.SMEM)
    vmem = pl.BlockSpec(memory_space=pltpu.VMEM)
    return pl.pallas_call(
        kernel,
        out_shape=jax.ShapeDtypeStruct(out_shape, F32),
        in_specs=[smem, smem, vmem, vmem],
        out_specs=vmem,
        scratch_shapes=scratch,
        compiler_params=pltpu.CompilerParams(vmem_limit_bytes=VMEM_BYTES),
        cost_estimate=pl.CostEstimate(flops=flops, bytes_accessed=4 << 20, transcendentals=0),
    )(*args)


MESH = pl.DeviceIdType.MESH
CHUNKS = 4


def fused_kernel(
    scale, total, pairs, x, w, cot,
    act, own_out, other_out, wg_out,
    x_hi, x_lo, a_all, part, dx, dy, rx, ry, h, h_all, gp, rl, rr, ga,
    wall, w_hi, w_lo, wt_hi, wt_lo, wterm, wpeer, wsum, wrecv,
    d_s, d_r, p_s, p_r, ag_s, ag_r, rs_s, rs_r, t_s, t_r,
    w_s, w_r, wp_s, wp_r, wg_s, wg_r, out_s, out_r, *tables,
):
    row, n, z = lax.axis_index("row"), lax.axis_index("nbr"), lax.axis_index("feat")
    col, line = lax.rem(n, 2), n // 2
    nx, ny, nd = line * 2 + (1 - col), (1 - line) * 2 + col, 3 - n
    peer = 1 - row
    right, left = jnp.minimum(z + 1, 3), jnp.maximum(z - 1, 0)
    half = TILE // 2
    owners = (nd, nx, ny, n)

    def send(src, dst, s_sem, r_sem, **to):
        return pltpu.make_async_remote_copy(
            src_ref=src, dst_ref=dst, send_sem=s_sem, recv_sem=r_sem,
            device_id=to, device_id_type=MESH,
        )

    def copy_diag(k, way):
        rows = pl.ds(way * half, half)
        return send(part.at[k, 0, rows], (dx, dy)[way].at[k], d_s.at[k, way], d_r.at[k, way],
                    nbr=(nx, ny)[way])

    def copy_part(k, way):
        return send(part.at[k, 1 + way], (rx, ry)[way].at[k], p_s.at[k, way], p_r.at[k, way],
                    nbr=(nx, ny)[way])

    def copy_hidden(k, block, step, way):
        return send(h.at[k, block], h.at[k, block], ag_s.at[k, way * 3 + step], ag_r.at[k, block],
                    feat=(right, left)[way])

    def copy_sum(k, block, step, way):
        buffer = (rl, rr)[way]
        return send(buffer.at[k, block], buffer.at[k, block], rs_s.at[k, way * 3 + step],
                    rs_r.at[k, way * 4 + block], feat=(right, left)[way])

    def copy_grad(k, way):
        return send(ga.at[k, 3], ga.at[k, 1 + way], t_s.at[k, way], t_r.at[k, way], nbr=(nx, ny)[way])

    def copy_on(k, way):
        rows = pl.ds(way * half, half)
        return send(ga.at[k, 1 + way, rows], ga.at[k, 0, rows], t_s.at[k, 2 + way], t_r.at[k, 2 + way],
                    nbr=(ny, nx)[way])

    def copy_weight(j, source):
        return send(w, wall.at[row * 4 + source], w_s.at[j], w_r.at[source], nbr=owners[j])

    def copy_weight_peer(m, side):
        return send(wall.at[side * 4 + m], wall.at[side * 4 + m], wp_s.at[m], wp_r.at[m], row=peer)

    def copy_terms():
        return send(wterm.at[pl.ds(peer * 4, 4)], wpeer, wg_s.at[3], wg_r.at[4], row=peer)

    def copy_wsum(j, source):
        return send(wsum.at[owners[j]], wrecv.at[source], wg_s.at[j], wg_r.at[source], nbr=owners[j])

    piece = own_out.shape[1] // 4

    def copy_out(j):
        cols = pl.ds(j * piece, piece)
        return send(own_out.at[:, cols], other_out.at[:, cols], out_s.at[j], out_r.at[j], row=peer)

    barrier = pltpu.get_barrier_semaphore()
    for target in (nx, ny, nd):
        pl.semaphore_signal(barrier, inc=1, device_id={"nbr": target}, device_id_type=MESH)
    pl.semaphore_signal(barrier, inc=1, device_id={"row": peer}, device_id_type=MESH)

    @pl.when(z > 0)
    def _():
        pl.semaphore_signal(barrier, inc=1, device_id={"feat": left}, device_id_type=MESH)

    @pl.when(z < 3)
    def _():
        pl.semaphore_signal(barrier, inc=1, device_id={"feat": right}, device_id_type=MESH)

    edge_setup(row, n, pairs, total[0], *tables)
    upper, lower = halves(x[...].T)
    x_hi[...] = upper
    x_lo[...] = lower
    wall[row * 4 + n] = w[...]
    wterm[...] = jnp.zeros_like(wterm)
    own_out[...] = jnp.zeros_like(own_out)
    pl.semaphore_wait(barrier, 4 + jnp.where(z > 0, 1, 0) + jnp.where(z < 3, 1, 0))

    def product(k, side):
        first = 4 * side * TILE
        upper, lower = pl.ds(first, 2 * TILE), pl.ds(first + 2 * TILE, 2 * TILE)
        for place in range(2):
            block = owners[2 * side + place] * CHUNKS + k
            fill(a_all.at[k, upper], a_all.at[k, lower], block, place * TILE, tables)
        both = dot(a_all[k, pl.ds(first, 4 * TILE), :], x_hi[...])
        value = both[: 2 * TILE] + (both[2 * TILE :] + dot(a_all[k, upper, :], x_lo[...]))
        part[k, 2 * side] = value[:TILE]
        part[k, 2 * side + 1] = value[TILE:]

    def gather_step(k, step):
        @pl.when(z >= step)
        def _():
            copy_hidden(k, z - step, 0, 0).wait_recv()
            if step < 3:
                @pl.when(z < 3)
                def _():
                    copy_hidden(k, z - step, step, 0).start()

        @pl.when(z <= 3 - step)
        def _():
            copy_hidden(k, z + step, 0, 1).wait_recv()
            if step < 3:
                @pl.when(z > 0)
                def _():
                    copy_hidden(k, z + step, step, 1).start()

    def sum_step(k, step):
        @pl.when((z >= 1) & (z <= 2) & (z <= step))
        def _():
            block = 3 - step + z
            copy_sum(k, block, 0, 0).wait_recv()
            rl[k, block] += gp[block]
            copy_sum(k, block, step - z, 0).start()

        @pl.when((z >= 1) & (z <= 2) & (3 - z <= step))
        def _():
            block = step + z - 3
            copy_sum(k, block, 0, 1).wait_recv()
            rr[k, block] += gp[block]
            copy_sum(k, block, step - 3 + z, 1).start()

    def dense(k):
        rows = pl.ds(pl.multiple_of(k * TILE, TILE), TILE)
        wide = h_all.shape[1] // 4
        for block in range(4):
            cols = slice(block * wide, (block + 1) * wide)
            h_all[:TILE, cols], h_all[TILE:, cols] = halves(h[k, block])
        both = dot(h_all[...], w_hi[...])
        pre = both[:TILE] + (both[TILE:] + dot(h_all[:TILE, :], w_lo[...]))
        squash = jax.nn.sigmoid(pre)
        act[rows, :] = pre * squash
        grad_pre = cot[rows, :] * squash * (1.0 + pre * (1.0 - squash))
        g_hi, g_lo = halves(grad_pre)
        both = dot(jnp.concatenate([g_hi, g_lo], axis=0), wt_hi[...])
        terms = both[:TILE] + (both[TILE:] + dot(g_hi, wt_lo[...]))
        for block in range(4):
            gp[block] = terms[:, block * wide : (block + 1) * wide]

        @pl.when(z == 0)
        def _():
            for step in range(3):
                rl[k, 3 - step] = gp[3 - step]
                copy_sum(k, 3 - step, step, 0).start()

        @pl.when(z == 3)
        def _():
            for step in range(3):
                rr[k, step] = gp[step]
                copy_sum(k, step, step, 1).start()

        g_hi, g_lo = halves(grad_pre.T)
        terms = dot(jnp.concatenate([g_hi, g_hi], axis=1), h_all[...]) + dot(g_lo, h_all[:TILE, :])
        for block in range(8):
            wterm[block] += terms[:, block * TILE : (block + 1) * TILE]

    def back_product(k, last, pieces):
        grads = ga[k].reshape(4 * TILE, ga.shape[3])
        g_hi, g_lo = halves(grads.T * scale)
        first, second = g_hi[:, : 2 * TILE], g_hi[:, 2 * TILE :]
        doubled = jnp.concatenate([first, first, second, second], axis=1)
        for j in pieces:
            cols = slice(j * piece, (j + 1) * piece)
            own_out[:, cols] += dot(doubled, a_all[k, :, cols]) + (
                dot(g_lo[:, : 2 * TILE], a_all[k, : 2 * TILE, cols])
                + dot(g_lo[:, 2 * TILE :], a_all[k, 4 * TILE : 6 * TILE, cols])
            )

            @pl.when(last)
            def _():
                copy_out(j).start()

    def advance(turn, carry):
        f, m, s, b = turn, turn - 1, turn - 2, turn - 3
        do_f, do_m = turn < 4, (turn >= 1) & (turn < 5)
        do_s, do_b = (turn >= 2) & (turn < 6), turn >= 3

        @pl.when(do_b)
        def _():
            for way in range(2):
                copy_grad(b, way).wait_recv()
                copy_on(b, way).start()

        @pl.when(do_f)
        def _():
            product(f, 0)
            copy_diag(f, 0).start()
            copy_diag(f, 1).start()

        @pl.when(turn == 1)
        def _():
            copy_weight_peer(n, row).start()
            for j in range(3):
                copy_weight(j, owners[j]).wait_recv()
                copy_weight_peer(owners[j], row).start()

        @pl.when(do_s)
        def _():
            sum_step(s, 1)

        @pl.when(do_m)
        def _():
            gather_step(m, 1)

        @pl.when(do_f)
        def _():
            product(f, 1)
            for way in range(2):
                copy_diag(f, way).wait_recv()
            part[f, 1, half:, :] += dy[f]
            copy_part(f, 0).start()
            part[f, 2, :half, :] += dx[f]
            copy_part(f, 1).start()

        @pl.when(turn == 0)
        def _():
            for j in range(3):
                copy_weight(j, n).start()

        @pl.when(do_b)
        def _():
            for way in range(2):
                copy_on(b, way).wait_recv()
            back_product(b, turn == 6, (0, 1))

        @pl.when(do_s)
        def _():
            sum_step(s, 2)

        @pl.when(do_m)
        def _():
            gather_step(m, 2)

        @pl.when(turn == 1)
        def _():
            for m_ in range(4):
                copy_weight_peer(m_, peer).wait_recv()
            whole = wall[...].reshape(w_hi.shape)
            w_hi[...], w_lo[...] = halves(whole)
            wt_hi[...], wt_lo[...] = halves(whole.T)

        @pl.when(do_b)
        def _():
            back_product(b, turn == 6, (2, 3))

        @pl.when(turn == 5)
        def _():
            copy_terms().wait_recv()
            wsum[...] = wterm[pl.ds(row * 4, 4)] + wpeer[...]
            for j in range(3):
                copy_wsum(j, n).start()

        @pl.when(do_f)
        def _():
            for way in range(2):
                copy_part(f, way).wait_recv()
            h[f, z] = (part[f, 3] + rx[f] + ry[f]) * scale

            @pl.when(z < 3)
            def _():
                copy_hidden(f, z, 0, 0).start()

            @pl.when(z > 0)
            def _():
                copy_hidden(f, z, 0, 1).start()

        @pl.when(do_s)
        def _():
            ga[s, 3] = gp[z]

            @pl.when(z > 0)
            def _():
                copy_sum(s, z, 0, 0).wait_recv()
                ga[s, 3] += rl[s, z]

            @pl.when(z < 3)
            def _():
                copy_sum(s, z, 0, 1).wait_recv()
                ga[s, 3] += rr[s, z]

            for way in range(2):
                copy_grad(s, way).start()

        @pl.when(do_m)
        def _():
            gather_step(m, 3)
            dense(m)

        @pl.when(turn == 4)
        def _():
            copy_terms().start()

        return carry

    lax.fori_loop(0, 7, advance, 0)

    for j in range(3):
        copy_wsum(j, owners[j]).wait_recv()
    wg_out[...] = (wsum[n] + wrecv[nx] + wrecv[ny] + wrecv[nd]).T
    for j in range(3):
        copy_weight(j, n).wait_send()
        copy_wsum(j, n).wait_send()
    copy_terms().wait_send()
    for m_ in range(4):
        copy_weight_peer(m_, row).wait_send()

    def settle(k, carry):
        for way in range(2):
            copy_diag(k, way).wait_send()
            copy_part(k, way).wait_send()
            copy_grad(k, way).wait_send()
            copy_on(k, way).wait_send()
        for step in range(3):
            @pl.when((z >= step) & (z < 3))
            def _():
                copy_hidden(k, z - step, step, 0).wait_send()

            @pl.when((z <= 3 - step) & (z > 0))
            def _():
                copy_hidden(k, z + step, step, 1).wait_send()

            @pl.when(step < 3 - z)
            def _():
                copy_sum(k, 3, step, 0).wait_send()

            @pl.when(step < z)
            def _():
                copy_sum(k, 0, step, 1).wait_send()
        return carry

    lax.fori_loop(0, CHUNKS, settle, 0)
    for j in range(4):
        copy_out(j).wait_send()
        copy_out(j).wait_recv()


def fused(features, pairs, total, weight, cotangent, scale):
    width, c_dev = features.shape
    full = 4 * width
    r_dev = cotangent.shape[0] * 4
    block = (CHUNKS, 4, TILE, width)
    smem = pl.BlockSpec(memory_space=pltpu.SMEM)
    vmem = pl.BlockSpec(memory_space=pltpu.VMEM)
    dma = pltpu.SemaphoreType.DMA
    scratch = [
        pltpu.VMEM((c_dev, width), BF16), pltpu.VMEM((c_dev, width), BF16),
        pltpu.VMEM((CHUNKS, 8 * TILE, c_dev), BF16),
        pltpu.VMEM(block, F32),
        pltpu.VMEM((CHUNKS, TILE // 2, width), F32), pltpu.VMEM((CHUNKS, TILE // 2, width), F32),
        pltpu.VMEM((CHUNKS, TILE, width), F32), pltpu.VMEM((CHUNKS, TILE, width), F32),
        pltpu.VMEM(block, F32),
        pltpu.VMEM((2 * TILE, full), BF16),
        pltpu.VMEM(block[1:], F32),
        pltpu.VMEM(block, F32), pltpu.VMEM(block, F32), pltpu.VMEM(block, F32),
        pltpu.VMEM((8, full // 8, width), F32),
        pltpu.VMEM((full, width), BF16), pltpu.VMEM((full, width), BF16),
        pltpu.VMEM((width, full), BF16), pltpu.VMEM((width, full), BF16),
        pltpu.VMEM((8, width, full // 8), F32),
        pltpu.VMEM((4, width, full // 8), F32), pltpu.VMEM((4, width, full // 8), F32),
        pltpu.VMEM((4, width, full // 8), F32),
        dma((CHUNKS, 2)), dma((CHUNKS, 2)), dma((CHUNKS, 2)), dma((CHUNKS, 2)),
        dma((CHUNKS, 6)), dma((CHUNKS, 4)), dma((CHUNKS, 6)), dma((CHUNKS, 8)),
        dma((CHUNKS, 4)), dma((CHUNKS, 4)),
        dma((3,)), dma((4,)), dma((4,)), dma((4,)), dma((4,)), dma((5,)), dma((4,)), dma((4,)),
    ] + table_shapes(r_dev, c_dev)
    shape = lambda *dims: jax.ShapeDtypeStruct(dims, F32)
    act, own, other, wg = pl.pallas_call(
        functools.partial(fused_kernel, scale),
        out_shape=[shape(*cotangent.shape), shape(width, c_dev), shape(width, c_dev), shape(*weight.shape)],
        in_specs=[smem, vmem, vmem, vmem, vmem],
        out_specs=[vmem, vmem, pl.BlockSpec(memory_space=pl.ANY), vmem],
        scratch_shapes=scratch,
        compiler_params=pltpu.CompilerParams(
            collective_id=0, has_side_effects=True, vmem_limit_bytes=VMEM_BYTES
        ),
        cost_estimate=pl.CostEstimate(
            flops=12 * r_dev * c_dev * width, bytes_accessed=16 << 20, transcendentals=cotangent.size
        ),
    )(total, pairs, features, weight, cotangent)
    return act, own + other, wg


def per_device(features, tile_list, tile_count, weight, cotangent):
    pairs = tile_list[0, 0]
    n_nbr = lax.axis_size("nbr")
    width, c_dev = features.shape
    r_dev = cotangent.shape[0] * n_nbr
    scale = (12.0 / (c_dev * n_nbr / 2)) ** 0.5 / modulus
    ids = jnp.stack([lax.axis_index("row"), lax.axis_index("nbr")]).astype(I32)
    total = tile_count[0]
    sizes = (lax.axis_size("row"), n_nbr, lax.axis_size("feat"))
    if sizes == (2, 4, 4) and width % TILE == 0 and r_dev == 16 * TILE and weight.shape[0] == TILE:
        return fused(features, pairs, total, weight, cotangent, scale)
    tables = table_shapes(r_dev, c_dev)
    flops = 6 * r_dev * c_dev * width
    adjacency = [pltpu.VMEM((256, c_dev), BF16)] * 2
    partial_value = local_call(
        functools.partial(forward_kernel, scale),
        (r_dev, width),
        [pltpu.VMEM((c_dev, width), BF16)] * 2 + adjacency + tables,
        (ids, total, pairs, features),
        flops,
    )
    hidden = lax.psum_scatter(partial_value, "nbr", scatter_dimension=0, tiled=True)
    weight_cols = lax.all_gather(weight, ("row", "nbr"), axis=0, tiled=True)
    hidden_all = lax.all_gather(hidden, "feat", axis=1, tiled=True)
    pre_act = jnp.dot(hidden_all, weight_cols, precision=high)
    squash = jax.nn.sigmoid(pre_act)
    activations = pre_act * squash
    grad_pre = cotangent * squash * (1.0 + pre_act * (1.0 - squash))
    grad_hidden = lax.psum_scatter(
        jnp.dot(grad_pre, weight_cols.T, precision=high), "feat", scatter_dimension=1, tiled=True
    )
    weight_terms = jnp.dot(hidden_all.T, grad_pre, precision=high)
    weight_grad = lax.psum_scatter(weight_terms, ("row", "nbr"), scatter_dimension=0, tiled=True)
    grad_block = lax.all_gather(grad_hidden, "nbr", axis=0, tiled=True)
    column_part = local_call(
        functools.partial(backward_kernel, scale),
        (width, c_dev),
        adjacency + tables,
        (ids, total, pairs, grad_block),
        flops,
    )
    feature_grad = lax.psum(column_part, "row")
    return (activations, feature_grad, weight_grad)


def solution(mesh):
    in_specs = (
        P("feat", "nbr"),
        P("row", "nbr", None, None),
        P("row", "nbr"),
        P(("row", "nbr"), "feat"),
        P(("row", "nbr"), "feat"),
    )
    out_specs = (P(("row", "nbr"), "feat"), P("feat", "nbr"), P(("row", "nbr"), "feat"))
    return jax.shard_map(
        per_device, mesh=mesh, in_specs=in_specs, out_specs=out_specs, check_vma=False
    )
```
